32 devices in a mesh: groups: 2 (over y), dom: 4 (over z), case: 2 (over x), sub: 2 (over core).
Axes of the slice: x: 2, y: 2, z: 4, core: 2. Of those that a mesh axis runs over, the one named last changes fastest.
Arguments:
- node_feats: bfloat16 [4, 5120, 128], P(('groups', 'case'), 'dom'), parts along dimension 0, may hold values from -6 to 6
- cotangent: bfloat16 [4, 5120, 128], P(('groups', 'case'), 'dom'), parts along dimension 0, may hold values from -6 to 6
- block_counts: int32 [8], P(('groups', 'dom')), parts along dimension 0, may hold values from 2 to 10, as said below
- neighbours: int32 [80, 8], P(('groups', 'dom')), parts along dimension 0, may hold values from -1 to 17, as said below
- send_sets: int32 [32, 2], P(('groups', 'dom')), parts along dimension 0, may hold values from 0 to 9, as said below
- edge_w1: bfloat16 [256, 512], P(None, 'sub'), may hold values from -0.375 to 0.375
- edge_b1: float32 [512], P('sub'), may hold values from -3 to 3
- edge_w2: bfloat16 [512, 128], P('sub'), may hold values from -0.25 to 0.25
- node_w1: bfloat16 [256, 512], P(None, 'sub'), may hold values from -0.375 to 0.375
- node_b1: float32 [512], P('sub'), may hold values from -3 to 3
- node_w2: bfloat16 [512, 128], P('sub'), may hold values from -0.25 to 0.25
- norm_gain: float32 [128], replicated, may hold values from 0.5 to 2
Outputs:
- new_nodes: bfloat16 [4, 5120, 128], P(('groups', 'case'), 'dom'), parts along dimension 0
- node_grads: bfloat16 [4, 5120, 128], P(('groups', 'case'), 'dom'), parts along dimension 0
- d_edge_w1: float32 [512, 512], P('groups', 'sub'), parts along dimension 0
- d_edge_b1: float32 [1024], P(('groups', 'sub')), parts along dimension 0
- d_edge_w2: float32 [1024, 128], P(('groups', 'sub')), parts along dimension 0
- d_node_w1: float32 [512, 512], P('groups', 'sub'), parts along dimension 0
- d_node_b1: float32 [1024], P(('groups', 'sub')), parts along dimension 0
- d_node_w2: float32 [1024, 128], P(('groups', 'sub')), parts along dimension 0
- d_norm_gain: float32 [256], P('groups'), parts along dimension 0
The draws below stay inside these ranges and needn't reach their ends.
There are 2 independent parts, one for each index of `groups`. The reference program is written for one: setup_inputs(seed, part) draws one part's arguments, and reference() takes and returns one part's arrays. A program takes and returns all parts, laid end to end along the dimension named above; an argument that names none is the same for every part. Nothing has to cross between parts.
Inputs may be any that keep to these rules, and one draw needn't show every extreme that they name: Blocks from block_counts[p] on are empty slots of partition p; some partition has 10 live blocks and some has 2. `neighbours`: row p * 10 + b lists the blocks that send to live block b of partition p: a value below 10 is a live block of p other than b, a value 10 + j * 2 + m is ghost slot j * 2 + m as in the reference program. Every entry of an empty block is -1 and no entry of a live block is. `send_sets`: row 4 p + j lists live blocks of partition p, repeats allowed, that partition p + d_j with d = (1, -1, 2, -2) receives.
All inputs are finite; a program needn't handle non-finite values.
Results may differ from the reference program's by a relative error of at most 0.009.
Values may be sent and summed in bfloat16 or wider, within the bound.
A program may use at most 64 MiB of HBM per device.

```python
import math
import jax
import jax.numpy as jnp
from jax import lax

F = 128
H = 512
BLOCK = 128
K = 8
BB = 2
NB = 10
NPART = 4
CASES = 2


def shared_counts(key):
    count_key = jax.random.fold_in(key, 101)
    base = jax.random.randint(count_key, (NPART,), 2, NB + 1)
    order = jax.random.permutation(jax.random.fold_in(count_key, 7), NPART)
    base = base.at[order[0]].set(NB)
    base = base.at[order[1]].set(2)
    return base.astype(jnp.int32)


def draw_block_counts(key, part):
    return shared_counts(key)


def draw_neighbours(key, part):
    counts = shared_counts(key)
    key = jax.random.fold_in(key, 3)
    key_step, key_ghost, key_pick = jax.random.split(key, 3)
    block_ids = jnp.arange(NB, dtype=jnp.int32)[None, :, None]
    limit = counts[:, None, None]
    step_draw = jax.random.randint(key_step, (NPART, NB, K), 0, NB)
    local_ids = (block_ids + 1 + step_draw % jnp.maximum(limit - 1, 1)) % limit
    ghost_ids = NB + jax.random.randint(key_ghost, (NPART, NB, K), 0, 4 * BB)
    picked = jax.random.randint(key_pick, (NPART, NB, K), 0, 2)
    link_ids = jnp.where(picked == 1, ghost_ids, local_ids)
    link_ids = jnp.where(block_ids < limit, link_ids, -1)
    fullest = jnp.argmax((counts == NB).astype(jnp.int32))
    link_ids = link_ids.at[fullest, 0, 0].set(NB + 4 * BB - 1)
    return link_ids.reshape(NPART * NB, K).astype(jnp.int32)


def draw_send_sets(key, part):
    counts = shared_counts(key)
    key = jax.random.fold_in(key, 5)
    raw_ids = jax.random.randint(key, (NPART, 4, BB), 0, NB)
    chosen = raw_ids % counts[:, None, None]
    fullest = jnp.argmax((counts == NB).astype(jnp.int32))
    smallest = jnp.argmax((counts == 2).astype(jnp.int32))
    chosen = chosen.at[fullest, 0, 0].set(NB - 1)
    chosen = chosen.at[smallest, 0, 0].set(0)
    return chosen.reshape(NPART * 4, BB).astype(jnp.int32)


def level_of(own_key, dims, cuts, low, largest):
    factor_of = 1.0
    for axis_at, shards_of in cuts:
        steps = jax.random.uniform(jax.random.fold_in(jax.random.fold_in(own_key, 6), axis_at), (shards_of,), jnp.float32, low / len(cuts), largest / len(cuts))
        factor_of = factor_of * jnp.repeat(jnp.exp(steps), dims[axis_at] // shards_of).reshape((-1,) + (1,) * (len(dims) - 1 - axis_at))
    return factor_of


def gaussian(own_key, dims, scale, bound, cuts=(), kind=jnp.bfloat16):
    level = level_of(own_key, dims, cuts, -0.22, 0.18) if cuts else 1.0
    drawn = jax.random.normal(own_key, dims, jnp.float32) * scale * level
    return jnp.minimum(jnp.maximum(drawn, -bound), bound).astype(kind)


def setup_inputs(seed: int = 0, part: int = 0) -> dict:
    seeds = jax.random.split(jax.random.key(seed), 13)
    part_keys = jax.random.split(jax.random.fold_in(seeds[12], part), 13)
    return {
        "node_feats": gaussian(part_keys[0], (CASES, NPART * NB * BLOCK, F), 1.0, 6.0, ((0, 2), (1, 4))),
        "cotangent": gaussian(part_keys[1], (CASES, NPART * NB * BLOCK, F), 1.0, 6.0, ((0, 2), (1, 4))),
        "block_counts": draw_block_counts(jax.random.fold_in(jax.random.fold_in(seeds[12], part), 71), part),
        "neighbours": draw_neighbours(jax.random.fold_in(jax.random.fold_in(seeds[12], part), 71), part),
        "send_sets": draw_send_sets(jax.random.fold_in(jax.random.fold_in(seeds[12], part), 71), part),
        "edge_w1": gaussian(seeds[5], (2 * F, H), (2 * F) ** -0.5, 0.375, ((1, 2),)),
        "edge_b1": gaussian(seeds[6], (H,), 0.5, 3.0, ((0, 2),), jnp.float32),
        "edge_w2": gaussian(seeds[7], (H, F), H ** -0.5, 0.25, ((0, 2),)),
        "node_w1": gaussian(seeds[8], (2 * F, H), (2 * F) ** -0.5, 0.375, ((1, 2),)),
        "node_b1": gaussian(seeds[9], (H,), 0.5, 3.0, ((0, 2),), jnp.float32),
        "node_w2": gaussian(seeds[10], (H, F), H ** -0.5, 0.25, ((0, 2),)),
        "norm_gain": jnp.clip(jnp.exp(jax.random.uniform(seeds[11], (F,), jnp.float32, math.log(0.5), math.log(2.0))), 0.5, 2.0),
    }


DISTANCES = (1, -1, 2, -2)
EPSILON = 1e-05

def silu_slope(values):
    sigmoid = jax.nn.sigmoid(values)
    return sigmoid * (1.0 + values * (1.0 - sigmoid))

def normalize(values, norm_gain):
    centre = lax.optimization_barrier(jnp.mean(values, axis=-1, keepdims=True))
    shifted = values - centre
    spread = lax.optimization_barrier(jnp.mean(shifted * shifted, axis=-1, keepdims=True))
    return shifted * lax.rsqrt(spread + EPSILON) * norm_gain

def one_case(node_feats, cotangent, block_counts, link_ids, send_sets, edge_w1, edge_b1, edge_w2, node_w1, node_b1, node_w2, norm_gain):
    features = node_feats.reshape(NPART, NB, BLOCK, F)
    part_ids = jnp.arange(NPART)
    ghosts = []
    for direction in range(4):
        distance = DISTANCES[direction]
        outgoing = features[part_ids[:, None], send_sets[:, direction]]
        rolled = jnp.roll(outgoing, distance, axis=0)
        inside = ((part_ids - distance >= 0) & (part_ids - distance < NPART)).astype(jnp.bfloat16)
        ghosts.append(rolled * inside[:, None, None, None])
    extended = jnp.concatenate([features] + ghosts, axis=1)
    alive_blocks = (jnp.arange(NB)[None, :] < block_counts[:, None]).astype(jnp.float32)
    edge_mask = ((link_ids >= 0) & (alive_blocks[:, :, None] > 0)).astype(jnp.float32)
    sources = extended[part_ids[:, None, None], jnp.maximum(link_ids, 0)]
    features32 = features.astype(jnp.float32)
    sources32 = sources.astype(jnp.float32)
    weight32 = edge_w1.astype(jnp.float32)
    pre_target = jnp.einsum('pbif,fh->pbih', features32, weight32[:F])
    pre_source = jnp.einsum('pbkif,fh->pbkih', sources32, weight32[F:])
    edge_preact = pre_source + pre_target[:, :, None] + edge_b1
    activation = jax.nn.silu(edge_preact) * edge_mask[..., None, None]
    edge_sum = lax.optimization_barrier(jnp.sum(activation, axis=2)).astype(jnp.bfloat16).reshape(-1, H)
    messages = jnp.dot(edge_sum, edge_w2, preferred_element_type=jnp.float32).astype(jnp.bfloat16)
    node_preact = jnp.dot(node_feats, node_w1[:F], preferred_element_type=jnp.float32) + jnp.dot(messages, node_w1[F:], preferred_element_type=jnp.float32) + node_b1
    node_hidden = jax.nn.silu(node_preact).astype(jnp.bfloat16)
    update = jnp.dot(node_hidden, node_w2, preferred_element_type=jnp.float32)
    alive_nodes = jnp.repeat(alive_blocks.reshape(-1), BLOCK)[:, None]
    normed, norm_back = jax.vjp(normalize, update, norm_gain)
    new_nodes = (node_feats.astype(jnp.float32) + alive_nodes * normed).astype(jnp.bfloat16)
    grad_normed = cotangent.astype(jnp.float32) * alive_nodes
    grad_update, d_norm_gain = norm_back(grad_normed)
    grad_update = grad_update.astype(jnp.bfloat16)
    grad_hidden = jnp.dot(grad_update, node_w2.T, preferred_element_type=jnp.float32)
    grad_node_pre = (grad_hidden * silu_slope(node_preact)).astype(jnp.bfloat16)
    d_node_w2 = jnp.dot(node_hidden.T, grad_update, preferred_element_type=jnp.float32)
    d_node_w1 = jnp.concatenate([jnp.dot(node_feats.T, grad_node_pre, preferred_element_type=jnp.float32), jnp.dot(messages.T, grad_node_pre, preferred_element_type=jnp.float32)], axis=0)
    d_node_b1 = lax.optimization_barrier(jnp.sum(grad_node_pre.astype(jnp.float32), axis=0))
    grad_x_node = jnp.dot(grad_node_pre, node_w1[:F].T, preferred_element_type=jnp.float32)
    grad_messages = jnp.dot(grad_node_pre, node_w1[F:].T, preferred_element_type=jnp.float32).astype(jnp.bfloat16)
    d_edge_w2 = jnp.dot(edge_sum.T, grad_messages, preferred_element_type=jnp.float32)
    grad_sum = jnp.dot(grad_messages, edge_w2.T, preferred_element_type=jnp.float32).reshape(NPART, NB, BLOCK, H)
    grad_edge_pre = (grad_sum[:, :, None] * silu_slope(edge_preact) * edge_mask[..., None, None]).astype(jnp.bfloat16)
    grad32 = grad_edge_pre.astype(jnp.float32)
    d_edge_w1 = jnp.concatenate([jnp.einsum('pbif,pbkih->fh', features32, grad32), jnp.einsum('pbkif,pbkih->fh', sources32, grad32)], axis=0)
    d_edge_b1 = lax.optimization_barrier(jnp.sum(grad32, axis=(0, 1, 2, 3)))
    target_grad = lax.optimization_barrier(jnp.sum(grad32, axis=2)).astype(jnp.bfloat16).reshape(-1, H)
    grad_x_target = jnp.dot(target_grad, edge_w1[:F].T, preferred_element_type=jnp.float32)
    grad_sources = jnp.einsum('pbkih,fh->pbkif', grad32, weight32[F:])
    extended_grad = jnp.zeros((NPART, NB + 4 * BB, BLOCK, F), jnp.float32)
    extended_grad = extended_grad.at[part_ids[:, None, None], jnp.maximum(link_ids, 0)].add(grad_sources)
    local_grad = extended_grad[:, :NB]
    for direction in range(4):
        distance = DISTANCES[direction]
        ghost_grad = extended_grad[:, NB + direction * BB:NB + (direction + 1) * BB]
        rolled = jnp.roll(ghost_grad, -distance, axis=0)
        inside = ((part_ids + distance >= 0) & (part_ids + distance < NPART)).astype(jnp.float32)
        local_grad = local_grad.at[part_ids[:, None], send_sets[:, direction]].add(rolled * inside[:, None, None, None])
    node_grads = (cotangent.astype(jnp.float32) + grad_x_node + grad_x_target + local_grad.reshape(-1, F)).astype(jnp.bfloat16)
    return (new_nodes, node_grads, d_edge_w1, d_edge_b1, d_edge_w2, d_node_w1, d_node_b1, d_node_w2, d_norm_gain)

def reference(node_feats, cotangent, block_counts, neighbours, send_sets, edge_w1, edge_b1, edge_w2, node_w1, node_b1, node_w2, norm_gain):
    link_ids = neighbours.reshape(NPART, NB, K)
    send_table = send_sets.reshape(NPART, 4, BB)

    def run_case(case_pair):
        return one_case(case_pair[0], case_pair[1], block_counts, link_ids, send_table, edge_w1, edge_b1, edge_w2, node_w1, node_b1, node_w2, norm_gain)
    results = lax.map(run_case, (node_feats, cotangent))
    totals = [lax.optimization_barrier(jnp.sum(entry, axis=0)) for entry in results[2:]]
    return (results[0], results[1], totals[0], totals[1], totals[2], totals[3], totals[4], totals[5], totals[6])
```

```python
import functools

import jax
import jax.numpy as jnp
from jax import lax
from jax.experimental import pallas as pl
from jax.experimental.pallas import tpu as pltpu
from jax.sharding import PartitionSpec as P

BLOCK = 128
CHUNK = 16
DISTANCES = (1, -1, 2, -2)
EPSILON = 1e-05
MESH = pl.DeviceIdType.MESH
BF = jnp.bfloat16
F32 = jnp.float32


def dot_nn(a, b):
    return lax.dot_general(a, b, (((1,), (0,)), ((), ())), preferred_element_type=F32)


def dot_nt(a, b):
    return lax.dot_general(a, b, (((1,), (1,)), ((), ())), preferred_element_type=F32)


def dot_tn(a, b):
    return lax.dot_general(a, b, (((0,), (0,)), ((), ())), preferred_element_type=F32)


def inside(position, count):
    return (position >= 0) & (position < count)


def remote(src, dst, send_sem, recv_sem, device):
    return pltpu.make_async_remote_copy(
        src_ref=src,
        dst_ref=dst,
        send_sem=send_sem,
        recv_sem=recv_sem,
        device_id=device,
        device_id_type=MESH,
    )


def gather_kernel(dom_count, bound, *refs):
    send, feats = refs[:2]
    mine = refs[2:8]
    ghosts = refs[8]
    others = refs[9:15]
    stage, half_send, half_recv, ghost_send, ghost_recv = refs[15:]
    here = lax.axis_index("dom")
    twin = {"sub": 1 - lax.axis_index("sub")}
    span = bound * BLOCK
    barrier = pltpu.get_barrier_semaphore()
    pl.semaphore_signal(barrier, inc=1, device_id=twin, device_id_type=MESH)
    expected = 1
    for distance in DISTANCES:
        there = here + distance
        present = inside(there, dom_count)
        expected = expected + jnp.where(present, 1, 0)

        @pl.when(present)
        def _():
            pl.semaphore_signal(barrier, inc=1, device_id={"dom": there}, device_id_type=MESH)

    for j in range(4):
        for m in range(bound):
            stage[j, m * BLOCK : (m + 1) * BLOCK, :] = feats[send[j, m]]
    pl.semaphore_wait(barrier, expected)

    def ghost_copy(j, there):
        return remote(
            stage.at[j],
            ghosts.at[pl.ds(j * span, span)],
            ghost_send.at[j],
            ghost_recv.at[j],
            {"dom": there},
        )

    for j in (2, 3, 0, 1):
        there = here + DISTANCES[j]

        @pl.when(inside(there, dom_count))
        def _():
            ghost_copy(j, there).start()

    halves = [
        remote(mine[n], others[n], half_send.at[n], half_recv.at[n], twin) for n in range(6)
    ]
    for copy in halves:
        copy.start()
    for j in range(4):

        @pl.when(jnp.logical_not(inside(here - DISTANCES[j], dom_count)))
        def _():
            ghosts[j * span : (j + 1) * span, :] = jnp.zeros((span, ghosts.shape[1]), BF)

    for copy in halves:
        copy.wait()
    for j in range(4):

        @pl.when(inside(here - DISTANCES[j], dom_count))
        def _():
            ghost_copy(j, here - DISTANCES[j]).wait_recv()

        @pl.when(inside(here + DISTANCES[j], dom_count))
        def _():
            ghost_copy(j, here + DISTANCES[j]).wait_send()


def layer_kernel(counts, links, feats, cot, ghosts, *refs):
    (ew1, oew1, eb1, oeb1, ew2, oew2, nw1, onw1, nb1, onb1, nw2, onw2, gain) = refs[:13]
    (new_o, part_o, ghost_o, mine_o, other_o) = refs[13:18]
    (
        w1h, w1f, w2f, n1f, n2f, psrc, ptgt, slope, gacc, gsum, esum, pair, hidden, gupd, gnode,
        gmsg, tgrad, gxnode, dsrc, dgain,
    ) = refs[18:]
    core = lax.axis_index("sub")
    block_count, fan = links.shape
    width = feats.shape[1]
    quarter = ew1.shape[1]
    own = block_count // 2
    ghost_count = ghosts.shape[0] // BLOCK

    def block_rows(b):
        return pl.ds(pl.multiple_of(b * BLOCK, BLOCK), BLOCK)

    w1f[:, :quarter] = ew1[...]
    w1f[:, quarter:] = oew1[...]
    w1h[...] = w1f[...] * jnp.asarray(0.5, BF)
    n1f[:, :quarter] = nw1[...]
    n1f[:, quarter:] = onw1[...]
    w2f[:quarter, :] = ew2[...]
    w2f[quarter:, :] = oew2[...]
    n2f[:quarter, :] = nw2[...]
    n2f[quarter:, :] = onw2[...]
    edge_bias = jnp.concatenate([eb1[...], oeb1[...]], axis=1) * 0.5
    node_bias = jnp.concatenate([nb1[...], onb1[...]], axis=1)
    gain_row = gain[...]
    dgain[...] = jnp.zeros_like(dgain)
    dsrc[...] = jnp.zeros_like(dsrc)

    @pl.loop(0, block_count)
    def _(b):
        psrc[b] = dot_nn(feats[block_rows(b), :], w1h[width:, :])
        gacc[b] = jnp.zeros(gacc.shape[1:], F32)

    @pl.loop(0, ghost_count)
    def _(b):
        psrc[block_count + b] = dot_nn(ghosts[block_rows(b), :], w1h[width:, :])
        gacc[block_count + b] = jnp.zeros(gacc.shape[1:], F32)

    @pl.loop(0, own)
    def _(i):
        b = core * own + i
        alive = jnp.where(b < counts[0], 1.0, 0.0)
        ids = [jnp.maximum(links[b, k], 0) for k in range(fan)]
        rows_i = block_rows(i)
        targets = feats[block_rows(b), :]
        ptgt[...] = dot_nn(targets, w1h[:width, :]) + edge_bias

        @pl.loop(0, BLOCK // CHUNK)
        def _(r):
            rows = pl.ds(pl.multiple_of(r * CHUNK, CHUNK), CHUNK)
            base = ptgt[rows, :]
            total = jnp.zeros_like(base)
            for k in range(fan):
                h = psrc[ids[k], rows, :] + base
                t = jnp.tanh(h)
                a = 1.0 + t
                q = h * a
                total = total + q
                slope[k, rows, :] = (a + q * (1.0 - t)).astype(BF)
            esum[pl.ds(pl.multiple_of(i * BLOCK + r * CHUNK, CHUNK), CHUNK), :] = (
                total * alive
            ).astype(BF)

        message = dot_nn(esum[rows_i, :], w2f[...]).astype(BF)
        pair[rows_i, :width] = targets
        pair[rows_i, width:] = message
        h = (dot_nn(pair[rows_i, :], n1f[...]) + node_bias) * 0.5
        t = jnp.tanh(h)
        a = 1.0 + t
        q = h * a
        node_slope = 0.5 * (a + q * (1.0 - t))
        hidden[rows_i, :] = q.astype(BF)
        update = dot_nn(hidden[rows_i, :], n2f[...])
        shifted = update - jnp.mean(update, axis=-1, keepdims=True)
        spread = jnp.mean(shifted * shifted, axis=-1, keepdims=True)
        scale = lax.rsqrt(spread + EPSILON)
        unit = shifted * scale
        new_o[rows_i, :] = (targets.astype(F32) + alive * (unit * gain_row)).astype(BF)
        seed = cot[block_rows(b), :].astype(F32) * alive
        dgain[...] += jnp.sum(seed * unit, axis=0, keepdims=True)
        seed = seed * gain_row
        grad = scale * (
            seed
            - jnp.mean(seed, axis=-1, keepdims=True)
            - unit * jnp.mean(seed * unit, axis=-1, keepdims=True)
        )
        gupd[rows_i, :] = grad.astype(BF)
        gnode[rows_i, :] = (dot_nt(gupd[rows_i, :], n2f[...]) * node_slope).astype(BF)
        back = dot_nt(gnode[rows_i, :], n1f[...])
        gxnode[rows_i, :] = back[:, :width] + cot[block_rows(b), :].astype(F32)
        gmsg[rows_i, :] = back[:, width:].astype(BF)
        gsum[...] = dot_nt(gmsg[rows_i, :], w2f[...]) * (0.5 * alive)

        @pl.loop(0, BLOCK // CHUNK)
        def _(r):
            rows = pl.ds(pl.multiple_of(r * CHUNK, CHUNK), CHUNK)
            upstream = gsum[rows, :]
            total = jnp.zeros_like(upstream)
            for k in range(fan):
                g = upstream * slope[k, rows, :].astype(F32)
                total = total + g
                gacc[ids[k], rows, :] += g
            tgrad[pl.ds(pl.multiple_of(i * BLOCK + r * CHUNK, CHUNK), CHUNK), :] = total.astype(BF)

    @pl.loop(0, block_count)
    def _(b):
        g = gacc[b].astype(BF)
        part_o[block_rows(b), :] = dot_nt(g, w1f[width:, :])
        dsrc[...] += dot_tn(feats[block_rows(b), :], g)

    @pl.loop(0, ghost_count)
    def _(b):
        g = gacc[block_count + b].astype(BF)
        ghost_o[block_rows(b), :] = dot_nt(g, w1f[width:, :]).astype(BF)
        dsrc[...] += dot_tn(ghosts[block_rows(b), :], g)

    @pl.loop(0, own)
    def _(i):
        rows = block_rows(core * own + i)
        rows_i = block_rows(i)
        part_o[rows, :] += gxnode[rows_i, :] + dot_nt(tgrad[rows_i, :], w1f[:width, :])

    own_feats = pair[:, :width]
    dtgt = dot_tn(own_feats, tgrad[...])
    dnode = dot_tn(pair[...], gnode[...])
    dew2 = dot_tn(esum[...], gmsg[...])
    dnw2 = dot_tn(hidden[...], gupd[...])
    ones = jnp.ones((16, own * BLOCK), BF)
    deb = dot_nn(ones, tgrad[...])[:1, :]
    dnb = dot_nn(ones, gnode[...])[:1, :]
    dgain_row = dgain[...].astype(BF).astype(F32)
    for out, lo in ((mine_o, 0), (other_o, quarter)):
        kind = out.dtype
        at = 0
        for c in range(lo, lo + quarter, 128):
            out[at : at + width, :] = dtgt[:, c : c + 128].astype(kind)
            out[at + width : at + 2 * width, :] = dsrc[:, c : c + 128].astype(kind)
            at += 2 * width
        for c in range(lo, lo + quarter, 128):
            out[at : at + 2 * width, :] = dnode[:, c : c + 128].astype(kind)
            at += 2 * width
        out[at : at + quarter, :] = dew2[lo : lo + quarter, :].astype(kind)
        at += quarter
        out[at : at + quarter, :] = dnw2[lo : lo + quarter, :].astype(kind)
        at += quarter
        lines = [deb[:, c : c + 128] for c in range(lo, lo + quarter, 128)]
        lines += [dnb[:, c : c + 128] for c in range(lo, lo + quarter, 128)]
        lines += [dgain_row]
        lines += [jnp.zeros((16 - len(lines), 128), F32)]
        out[at : at + 16, :] = jnp.concatenate(lines, axis=0).astype(kind)
        at += 16
        if at < out.shape[0]:
            out[at:, :] = jnp.zeros((out.shape[0] - at, 128), kind)


def reduce_kernel(dom_count, case_count, bound, *refs):
    send, part, ghost_grad, w_mine, w_other, new_mine = refs[:6]
    final, node_mine, node_other, new_other = refs[6:10]
    (
        ghost_in, twin_in, reduced, case_in, case_red, dom_in,
        twin_send, twin_recv, ghost_send, ghost_recv, case_send, case_recv,
        dom_send, dom_recv, gd_send, gd_recv, gc_send, gc_recv,
    ) = refs[10:]
    here = lax.axis_index("dom")
    case = lax.axis_index("case")
    twin = {"sub": 1 - lax.axis_index("sub")}
    span = bound * BLOCK
    total = w_mine.shape[0]
    slab = total // case_count
    piece = slab // dom_count
    block_count = part.shape[0] // BLOCK

    barrier = pltpu.get_barrier_semaphore()
    pl.semaphore_signal(barrier, inc=1, device_id=twin, device_id_type=MESH)
    for o in range(1, dom_count):
        pl.semaphore_signal(
            barrier, inc=1, device_id={"dom": lax.rem(here + o, dom_count)}, device_id_type=MESH
        )
    for o in range(1, case_count):
        pl.semaphore_signal(
            barrier, inc=1, device_id={"case": lax.rem(case + o, case_count)}, device_id_type=MESH
        )
    pl.semaphore_wait(barrier, 1 + (dom_count - 1) + (case_count - 1))

    twin_w = remote(w_other, twin_in, twin_send.at[0], twin_recv.at[0], twin)
    twin_w.start()

    def ghost_copy(j, there):
        return remote(
            ghost_grad.at[pl.ds(j * span, span)],
            ghost_in.at[pl.ds(j * span, span)],
            ghost_send.at[j],
            ghost_recv.at[j],
            {"dom": there},
        )

    for j in (2, 3, 0, 1):
        there = here - DISTANCES[j]

        @pl.when(inside(there, dom_count))
        def _():
            ghost_copy(j, there).start()

    twin_new = remote(new_mine, new_other, twin_send.at[1], twin_recv.at[1], twin)
    twin_new.start()
    for j in range(4):

        @pl.when(jnp.logical_not(inside(here + DISTANCES[j], dom_count)))
        def _():
            ghost_in[j * span : (j + 1) * span, :] = jnp.zeros((span, 128), BF)

    def slab_rows(c):
        return pl.ds(pl.multiple_of(c * slab, 16), slab)

    def piece_rows(d):
        return pl.ds(pl.multiple_of(d * piece, 16), piece)

    def final_rows(c, d):
        return pl.ds(pl.multiple_of(c * slab + d * piece, 16), piece)

    twin_w.wait()
    case_copies = []
    for o in range(1, case_count):
        peer = lax.rem(case + o, case_count)
        rows = slab_rows(peer)
        reduced[o - 1] = (w_mine[rows, :] + twin_in[rows, :].astype(F32)).astype(BF)
        copy = remote(
            reduced.at[o - 1],
            case_in.at[o - 1],
            case_send.at[o - 1],
            case_recv.at[o - 1],
            {"case": peer},
        )
        copy.start()
        case_copies.append(copy)

    for j in range(4):

        @pl.when(inside(here + DISTANCES[j], dom_count))
        def _():
            ghost_copy(j, here + DISTANCES[j]).wait_recv()

    hits = [
        [jnp.where(send[j, m] == b, 1.0, 0.0) for j in range(4) for m in range(bound)]
        for b in range(block_count)
    ]

    @pl.loop(0, BLOCK // CHUNK)
    def _(r):
        slots = [
            ghost_in[pl.ds(pl.multiple_of(s * BLOCK + r * CHUNK, CHUNK), CHUNK), :].astype(F32)
            for s in range(4 * bound)
        ]
        for b in range(block_count):
            rows = pl.ds(pl.multiple_of(b * BLOCK + r * CHUNK, CHUNK), CHUNK)
            value = part[rows, :]
            for s in range(4 * bound):
                value = value + hits[b][s] * slots[s]
            node_mine[rows, :] = value.astype(BF)

    twin_node = remote(node_mine, node_other, twin_send.at[2], twin_recv.at[2], twin)
    twin_node.start()

    for copy in case_copies:
        copy.wait()
    rows = slab_rows(case)
    value = w_mine[rows, :] + twin_in[rows, :].astype(F32)
    for o in range(1, case_count):
        value = value + case_in[o - 1].astype(F32)
    case_red[...] = value.astype(BF)
    dom_copies = []
    for o in range(1, dom_count):
        peer = lax.rem(here + o, dom_count)
        copy = remote(
            case_red.at[piece_rows(peer)],
            dom_in.at[o - 1],
            dom_send.at[o - 1],
            dom_recv.at[o - 1],
            {"dom": peer},
        )
        copy.start()
        dom_copies.append(copy)
    for copy in dom_copies:
        copy.wait()
    value = case_red[piece_rows(here), :].astype(F32)
    for o in range(1, dom_count):
        value = value + dom_in[o - 1].astype(F32)
    final[final_rows(case, here), :] = value.astype(BF)

    def dom_gather(o, owner, peer):
        rows = final_rows(case, owner)
        return remote(
            final.at[rows], final.at[rows], gd_send.at[o], gd_recv.at[o], {"dom": peer}
        )

    def case_gather(o, oz, source):
        rows = final_rows(source, lax.rem(here - oz + dom_count, dom_count))
        n = (o - 1) * dom_count + oz
        return remote(
            final.at[rows],
            final.at[rows],
            gc_send.at[n],
            gc_recv.at[n],
            {"case": lax.rem(case + o, case_count)},
        )

    for o in range(1, dom_count):
        dom_gather(o - 1, here, lax.rem(here + o, dom_count)).start()
    for oz in range(dom_count):
        if oz > 0:
            source = lax.rem(here - oz + dom_count, dom_count)
            dom_gather(oz - 1, source, source).wait_recv()
        for o in range(1, case_count):
            case_gather(o, oz, case).start()
    twin_new.wait()
    twin_node.wait()
    for j in range(4):

        @pl.when(inside(here - DISTANCES[j], dom_count))
        def _():
            ghost_copy(j, here - DISTANCES[j]).wait_send()

    for o in range(1, dom_count):
        dom_gather(o - 1, here, lax.rem(here + o, dom_count)).wait_send()
    for oz in range(dom_count):
        for o in range(1, case_count):
            case_gather(o, oz, case).wait_send()
            case_gather(o, oz, lax.rem(case - o + case_count, case_count)).wait_recv()


def unpack_kernel(final, node_mine, node_other, new_mine, new_other, *outs):
    new_nodes, node_grads, dew1, deb, dew2, dnw1, dnb, dnw2, dgain = outs
    core = lax.axis_index("sub")
    half = new_mine.shape[0]
    new_nodes[pl.ds(pl.multiple_of(core * half, BLOCK), half), :] = new_mine[...]
    new_nodes[pl.ds(pl.multiple_of((1 - core) * half, BLOCK), half), :] = new_other[...]
    node_grads[...] = (node_mine[...].astype(F32) + node_other[...].astype(F32)).astype(BF)
    at = 0
    tall = dew1.shape[0]
    quarter = dew1.shape[1]
    for out in (dew1, dnw1):
        for c in range(0, quarter, 128):
            out[:, c : c + 128] = final[at : at + tall, :].astype(F32)
            at += tall
    for out in (dew2, dnw2):
        out[...] = final[at : at + quarter, :].astype(F32)
        at += quarter
    tail = final[at : at + 16, :].astype(F32)
    n = quarter // 128
    for c in range(n):
        deb[:, c * 128 : (c + 1) * 128] = tail[c : c + 1, :]
        dnb[:, c * 128 : (c + 1) * 128] = tail[n + c : n + c + 1, :]
    dgain[...] = tail[2 * n : 2 * n + 1, :]


def on_device(
    dom_count,
    case_count,
    node_feats,
    cotangent,
    block_counts,
    neighbours,
    send_sets,
    edge_w1,
    edge_b1,
    edge_w2,
    node_w1,
    node_b1,
    node_w2,
    norm_gain,
):
    feats = node_feats[0]
    cot = cotangent[0]
    rows, width = feats.shape
    block_count, fan = neighbours.shape
    bound = send_sets.shape[1]
    quarter = edge_w1.shape[1]
    wide = 2 * quarter
    ghost_rows = 4 * bound * BLOCK
    ext_count = block_count + 4 * bound
    half = rows // 2
    vmem = pl.BlockSpec(memory_space=pltpu.VMEM)
    smem = pl.BlockSpec(memory_space=pltpu.SMEM)
    shape = jax.ShapeDtypeStruct
    dma = pltpu.SemaphoreType.DMA
    eb = edge_b1.reshape(1, quarter)
    nb = node_b1.reshape(1, quarter)
    gain = norm_gain.reshape(1, width)
    mine = (edge_w1, eb, edge_w2, node_w1, nb, node_w2)

    gathered = pl.pallas_call(
        functools.partial(gather_kernel, dom_count, bound),
        out_shape=[shape((ghost_rows, width), BF)] + [shape(m.shape, m.dtype) for m in mine],
        in_specs=[smem] + [vmem] * 7,
        out_specs=[vmem] * 7,
        scratch_shapes=[
            pltpu.VMEM((4, bound * BLOCK, width), BF),
            dma((6,)),
            dma((6,)),
            dma((4,)),
            dma((4,)),
        ],
        compiler_params=pltpu.CompilerParams(
            collective_id=0, has_side_effects=True, vmem_limit_bytes=16 << 20
        ),
        name="gather",
    )(send_sets, feats.reshape(block_count, BLOCK, width), *mine)
    ghosts = gathered[0]
    weights = []
    for m, other in zip(mine, gathered[1:]):
        weights += [m, other]

    own_rows = 6 * quarter + 16
    unit = 16 * dom_count * case_count
    total = -(-own_rows // unit) * unit
    slab = total // case_count
    piece = slab // dom_count

    new_mine, part, ghost_grad, w_mine, w_other = pl.pallas_call(
        layer_kernel,
        out_shape=[
            shape((half, width), BF),
            shape((rows, width), F32),
            shape((ghost_rows, width), BF),
            shape((total, 128), F32),
            shape((total, 128), BF),
        ],
        in_specs=[smem, smem] + [vmem] * 16,
        out_specs=[vmem] * 5,
        scratch_shapes=[
            pltpu.VMEM((2 * width, wide), BF),
            pltpu.VMEM((2 * width, wide), BF),
            pltpu.VMEM((wide, width), BF),
            pltpu.VMEM((2 * width, wide), BF),
            pltpu.VMEM((wide, width), BF),
            pltpu.VMEM((ext_count, BLOCK, wide), F32),
            pltpu.VMEM((BLOCK, wide), F32),
            pltpu.VMEM((fan, BLOCK, wide), BF),
            pltpu.VMEM((ext_count, BLOCK, wide), F32),
            pltpu.VMEM((BLOCK, wide), F32),
            pltpu.VMEM((half, wide), BF),
            pltpu.VMEM((half, 2 * width), BF),
            pltpu.VMEM((half, wide), BF),
            pltpu.VMEM((half, width), BF),
            pltpu.VMEM((half, wide), BF),
            pltpu.VMEM((half, width), BF),
            pltpu.VMEM((half, wide), BF),
            pltpu.VMEM((half, width), F32),
            pltpu.VMEM((width, wide), F32),
            pltpu.VMEM((1, width), F32),
        ],
        compiler_params=pltpu.CompilerParams(vmem_limit_bytes=40 << 20),
        name="layer",
    )(block_counts, neighbours, feats, cot, ghosts, *weights, gain)

    final, node_mine, node_other, new_other = pl.pallas_call(
        functools.partial(reduce_kernel, dom_count, case_count, bound),
        out_shape=[
            shape((total, 128), BF),
            shape((rows, width), BF),
            shape((rows, width), BF),
            shape((half, width), BF),
        ],
        in_specs=[smem] + [vmem] * 5,
        out_specs=[vmem] * 4,
        scratch_shapes=[
            pltpu.VMEM((ghost_rows, width), BF),
            pltpu.VMEM((total, 128), BF),
            pltpu.VMEM((case_count - 1, slab, 128), BF),
            pltpu.VMEM((case_count - 1, slab, 128), BF),
            pltpu.VMEM((slab, 128), BF),
            pltpu.VMEM((dom_count - 1, piece, 128), BF),
            dma((3,)),
            dma((3,)),
            dma((4,)),
            dma((4,)),
            dma((case_count - 1,)),
            dma((case_count - 1,)),
            dma((dom_count - 1,)),
            dma((dom_count - 1,)),
            dma((dom_count - 1,)),
            dma((dom_count - 1,)),
            dma(((case_count - 1) * dom_count,)),
            dma(((case_count - 1) * dom_count,)),
        ],
        compiler_params=pltpu.CompilerParams(
            collective_id=1, has_side_effects=True, vmem_limit_bytes=24 << 20
        ),
        name="reduce",
    )(send_sets, part, ghost_grad, w_mine, w_other, new_mine)

    outs = pl.pallas_call(
        unpack_kernel,
        out_shape=[
            shape((rows, width), BF),
            shape((rows, width), BF),
            shape((2 * width, quarter), F32),
            shape((1, quarter), F32),
            shape((quarter, width), F32),
            shape((2 * width, quarter), F32),
            shape((1, quarter), F32),
            shape((quarter, width), F32),
            shape((1, width), F32),
        ],
        in_specs=[vmem] * 5,
        out_specs=[vmem] * 9,
        compiler_params=pltpu.CompilerParams(vmem_limit_bytes=16 << 20),
        name="unpack",
    )(final, node_mine, node_other, new_mine, new_other)
    return (
        outs[0][None],
        outs[1][None],
        outs[2],
        outs[3].reshape(quarter),
        outs[4],
        outs[5],
        outs[6].reshape(quarter),
        outs[7],
        outs[8].reshape(width),
    )


def solution(mesh):
    placed = (
        P(("groups", "case"), "dom", None),
        P(("groups", "case"), "dom", None),
        P(("groups", "dom")),
        P(("groups", "dom"), None),
        P(("groups", "dom"), None),
        P(None, "sub"),
        P("sub"),
        P("sub", None),
        P(None, "sub"),
        P("sub"),
        P("sub", None),
        P(),
    )
    return jax.shard_map(
        functools.partial(on_device, mesh.shape["dom"], mesh.shape["case"]),
        mesh=mesh,
        in_specs=placed,
        out_specs=(
            P(("groups", "case"), "dom", None),
            P(("groups", "case"), "dom", None),
            P("groups", "sub"),
            P(("groups", "sub")),
            P(("groups", "sub"), None),
            P("groups", "sub"),
            P(("groups", "sub")),
            P(("groups", "sub"), None),
            P("groups"),
        ),
        check_vma=False,
    )
```

```python
import functools

import jax
import jax.numpy as jnp
from jax import lax
from jax.experimental import pallas as pl
from jax.experimental.pallas import tpu as pltpu
from jax.sharding import PartitionSpec as P

BLOCK = 128
CHUNK = 16
DISTANCES = (1, -1, 2, -2)
EPSILON = 1e-05
MESH = pl.DeviceIdType.MESH
BF = jnp.bfloat16
F32 = jnp.float32


def dot_nn(a, b):
    return lax.dot_general(a, b, (((1,), (0,)), ((), ())), preferred_element_type=F32)


def dot_nt(a, b):
    return lax.dot_general(a, b, (((1,), (1,)), ((), ())), preferred_element_type=F32)


def dot_tn(a, b):
    return lax.dot_general(a, b, (((0,), (0,)), ((), ())), preferred_element_type=F32)


def inside(position, count):
    return (position >= 0) & (position < count)


def remote(src, dst, send_sem, recv_sem, device):
    return pltpu.make_async_remote_copy(
        src_ref=src,
        dst_ref=dst,
        send_sem=send_sem,
        recv_sem=recv_sem,
        device_id=device,
        device_id_type=MESH,
    )


def chain_kernel(links, prev_o, last_o):
    core = lax.axis_index("sub")
    block_count, fan = links.shape
    own = block_count // 2
    none = own * fan

    @pl.loop(0, last_o.shape[0])
    def _(s):
        last_o[s] = none

    @pl.loop(0, none)
    def _(e):
        source = jnp.maximum(links[core * own + e // fan, lax.rem(e, fan)], 0)
        prev_o[e] = last_o[source]
        last_o[source] = e


class Reducer:
    def __init__(self, dom_count, case_count, final, refs):
        (self.mine, self.other, self.twin_in, self.reduced, self.case_in, self.case_red,
         self.dom_in, self.send, self.recv) = refs
        self.final = final
        self.dom_count, self.case_count = dom_count, case_count
        self.here, self.case = lax.axis_index("dom"), lax.axis_index("case")
        self.twin = {"sub": 1 - lax.axis_index("sub")}
        self.slab = self.mine.shape[0] // case_count
        self.piece = self.slab // dom_count

    def copy(self, src, dst, n, device):
        return remote(src, dst, self.send.at[n], self.recv.at[n], device)

    def slab_rows(self, c):
        return pl.ds(pl.multiple_of(c * self.slab, 16), self.slab)

    def piece_rows(self, d):
        return pl.ds(pl.multiple_of(d * self.piece, 16), self.piece)

    def final_rows(self, c, d):
        return pl.ds(pl.multiple_of(c * self.slab + d * self.piece, 16), self.piece)

    def case_peer(self, o):
        return lax.rem(self.case + o, self.case_count)

    def dom_peer(self, o):
        return lax.rem(self.here + o, self.dom_count)

    def sub_copy(self):
        return self.copy(self.other, self.twin_in, 0, self.twin)

    def case_copy(self, o):
        return self.copy(
            self.reduced.at[o - 1], self.case_in.at[o - 1], o, {"case": self.case_peer(o)}
        )

    def dom_copy(self, o):
        peer = self.dom_peer(o)
        return self.copy(
            self.case_red.at[self.piece_rows(peer)],
            self.dom_in.at[o - 1],
            self.case_count + o - 1,
            {"dom": peer},
        )

    def dom_gather(self, o, owner, peer):
        rows = self.final_rows(self.case, owner)
        n = self.case_count + self.dom_count - 1 + o - 1
        return self.copy(self.final.at[rows], self.final.at[rows], n, {"dom": peer})

    def case_gather(self, o, oz, source):
        owner = lax.rem(self.here - oz + self.dom_count, self.dom_count)
        rows = self.final_rows(source, owner)
        n = self.case_count + 2 * (self.dom_count - 1) + (o - 1) * self.dom_count + oz
        return self.copy(
            self.final.at[rows], self.final.at[rows], n, {"case": self.case_peer(o)}
        )

    def to_sub(self):
        self.sub_copy().start()

    def to_case(self):
        self.sub_copy().wait()
        for o in range(1, self.case_count):
            rows = self.slab_rows(self.case_peer(o))
            self.reduced[o - 1] = (self.mine[rows, :] + self.twin_in[rows, :].astype(F32)).astype(BF)
            self.case_copy(o).start()

    def to_dom(self):
        for o in range(1, self.case_count):
            self.case_copy(o).wait()
        rows = self.slab_rows(self.case)
        value = self.mine[rows, :] + self.twin_in[rows, :].astype(F32)
        for o in range(1, self.case_count):
            value = value + self.case_in[o - 1].astype(F32)
        self.case_red[...] = value.astype(BF)
        for o in range(1, self.dom_count):
            self.dom_copy(o).start()

    def to_gather(self):
        for o in range(1, self.dom_count):
            self.dom_copy(o).wait()
        value = self.case_red[self.piece_rows(self.here), :].astype(F32)
        for o in range(1, self.dom_count):
            value = value + self.dom_in[o - 1].astype(F32)
        self.final[self.final_rows(self.case, self.here), :] = value.astype(BF)
        for o in range(1, self.dom_count):
            self.dom_gather(o, self.here, self.dom_peer(o)).start()
        for o in range(1, self.case_count):
            self.case_gather(o, 0, self.case).start()

    def forward(self):
        for oz in range(1, self.dom_count):
            source = lax.rem(self.here - oz + self.dom_count, self.dom_count)
            self.dom_gather(oz, source, source).wait_recv()
            for o in range(1, self.case_count):
                self.case_gather(o, oz, self.case).start()

    def finish(self):
        for o in range(1, self.dom_count):
            self.dom_gather(o, self.here, self.dom_peer(o)).wait_send()
        for oz in range(self.dom_count):
            for o in range(1, self.case_count):
                self.case_gather(o, oz, self.case).wait_send()
                source = lax.rem(self.case - o + self.case_count, self.case_count)
                self.case_gather(o, oz, source).wait_recv()


def fill(out, pieces, lines):
    at = 0
    for piece in pieces:
        out[at : at + piece.shape[0], :] = piece.astype(out.dtype)
        at += piece.shape[0]
    lines = lines + [jnp.zeros((16 - len(lines), 128), F32)]
    out[at : at + 16, :] = jnp.concatenate(lines, axis=0).astype(out.dtype)
    at += 16
    if at < out.shape[0]:
        out[at:, :] = jnp.zeros((out.shape[0] - at, 128), out.dtype)


def columns(value, lo, hi):
    return [value[:, c : c + 128] for c in range(lo, hi, 128)]


def layer_kernel(dom_count, case_count, bound, *refs):
    send, counts, links, prev, last = refs[:5]
    feats_h, cot_h, gain_h = refs[5:8]
    mine = refs[8:14]
    final_n, final_e, node_mine, node_other, new_mine, new_other = refs[14:20]
    reducer_n = Reducer(dom_count, case_count, final_n, refs[20:29])
    reducer_e = Reducer(dom_count, case_count, final_e, refs[29:38])
    (
        feats, cot, gain, stage, ghosts, ext,
        w1f, ebias, w2f, n1f, nbias, n2f, w1h,
        psrc, ptgt, slope, gsum, esum, pair, hidden, gupd, gnode,
        gmsg, tgrad, gxnode, dsrc, dgain, srcs, chain, ghost_grad, ghost_in,
        local, half_send, half_recv, ghost_send, ghost_recv, home_send, home_recv,
        twin_send, twin_recv,
    ) = refs[38:]
    core = lax.axis_index("sub")
    here = lax.axis_index("dom")
    case = lax.axis_index("case")
    twin = {"sub": 1 - core}
    block_count, fan = links.shape
    width = feats.shape[2]
    quarter = mine[0].shape[1]
    wide = 2 * quarter
    own = block_count // 2
    ghost_count = 4 * bound
    none = own * fan
    left, right = pl.ds(0, quarter), pl.ds(quarter, quarter)

    def block_rows(b):
        return pl.ds(pl.multiple_of(b * BLOCK, BLOCK), BLOCK)

    def half_of(n, part):
        ref = (w1f, ebias, w2f, n1f, nbias, n2f)[n]
        return ref.at[part, :] if n in (2, 5) else ref.at[:, part]

    locals_ = [pltpu.make_async_copy(feats_h, feats, local.at[0])]
    locals_ += [pltpu.make_async_copy(mine[n], half_of(n, left), local.at[1 + n]) for n in range(6)]
    locals_ += [
        pltpu.make_async_copy(gain_h, gain, local.at[7]),
        pltpu.make_async_copy(cot_h, cot, local.at[8]),
    ]
    for copy in locals_:
        copy.start()

    barrier = pltpu.get_barrier_semaphore()
    pl.semaphore_signal(barrier, inc=1, device_id=twin, device_id_type=MESH)
    for o in range(1, dom_count):
        pl.semaphore_signal(
            barrier, inc=1, device_id={"dom": lax.rem(here + o, dom_count)}, device_id_type=MESH
        )
    for o in range(1, case_count):
        pl.semaphore_signal(
            barrier, inc=1, device_id={"case": lax.rem(case + o, case_count)}, device_id_type=MESH
        )
    locals_[0].wait()
    for j in range(4):
        for m in range(bound):
            stage[j, m] = feats[send[j, m]]
    pl.semaphore_wait(barrier, 1 + (dom_count - 1) + (case_count - 1))

    halves = [
        remote(mine[n], half_of(n, right), half_send.at[n], half_recv.at[n], twin)
        for n in range(6)
    ]
    halves[0].start()

    def ghost_copy(j, there):
        return remote(
            stage.at[j], ghosts.at[j], ghost_send.at[j], ghost_recv.at[j], {"dom": there}
        )

    for j in (2, 3, 0, 1):

        @pl.when(inside(here + DISTANCES[j], dom_count))
        def _():
            ghost_copy(j, here + DISTANCES[j]).start()

    for copy in halves[1:]:
        copy.start()
    for j in range(4):

        @pl.when(jnp.logical_not(inside(here - DISTANCES[j], dom_count)))
        def _():
            ghosts[j] = jnp.zeros(ghosts.shape[1:], BF)

        @pl.when(jnp.logical_not(inside(here + DISTANCES[j], dom_count)))
        def _():
            ghost_in[j] = jnp.zeros(ghost_in.shape[1:], BF)

    dgain[...] = jnp.zeros_like(dgain)
    dsrc[...] = jnp.zeros_like(dsrc)
    chain[none] = jnp.zeros(chain.shape[1:], F32)
    for copy in locals_[1:]:
        copy.wait()
    halves[0].wait()
    w1h[...] = w1f[...] * jnp.asarray(0.5, BF)

    @pl.loop(0, block_count)
    def _(b):
        ext[b] = feats[b]
        psrc[b] = dot_nn(feats[b], w1h[width:, :])

    for copy in halves[1:]:
        copy.wait()
    edge_bias = ebias[...] * 0.5
    node_bias = nbias[...]
    gain_row = gain[...]
    for j in range(4):

        @pl.when(inside(here - DISTANCES[j], dom_count))
        def _():
            ghost_copy(j, here - DISTANCES[j]).wait_recv()

        @pl.when(inside(here + DISTANCES[j], dom_count))
        def _():
            ghost_copy(j, here + DISTANCES[j]).wait_send()

        for m in range(bound):
            s = block_count + j * bound + m
            ext[s] = ghosts[j, m]
            psrc[s] = dot_nn(ghosts[j, m], w1h[width:, :])

    @pl.loop(0, own)
    def _(i):
        b = core * own + i
        alive = jnp.where(b < counts[0], 1.0, 0.0)
        ids = [jnp.maximum(links[b, k], 0) for k in range(fan)]
        rows_i = block_rows(i)
        targets = feats[b]
        ptgt[...] = dot_nn(targets, w1h[:width, :]) + edge_bias

        @pl.loop(0, BLOCK // CHUNK)
        def _(r):
            rows = pl.ds(pl.multiple_of(r * CHUNK, CHUNK), CHUNK)
            base = ptgt[rows, :]
            total = jnp.zeros_like(base)
            for k in range(fan):
                h = psrc[ids[k], rows, :] + base
                t = jnp.tanh(h)
                a = 1.0 + t
                q = h * a
                total = total + q
                at = pl.multiple_of((i * fan + k) * BLOCK + r * CHUNK, CHUNK)
                slope[pl.ds(at, CHUNK), :] = (a + q * (1.0 - t)).astype(BF)
            esum[pl.ds(pl.multiple_of(i * BLOCK + r * CHUNK, CHUNK), CHUNK), :] = (
                total * alive
            ).astype(BF)

        message = dot_nn(esum[rows_i, :], w2f[...]).astype(BF)
        pair[rows_i, :width] = targets
        pair[rows_i, width:] = message
        h = (dot_nn(pair[rows_i, :], n1f[...]) + node_bias) * 0.5
        t = jnp.tanh(h)
        a = 1.0 + t
        q = h * a
        node_slope = 0.5 * (a + q * (1.0 - t))
        hidden[rows_i, :] = q.astype(BF)
        update = dot_nn(hidden[rows_i, :], n2f[...])
        shifted = update - jnp.mean(update, axis=-1, keepdims=True)
        spread = jnp.mean(shifted * shifted, axis=-1, keepdims=True)
        scale = lax.rsqrt(spread + EPSILON)
        unit = shifted * scale
        new_mine[rows_i, :] = (targets.astype(F32) + alive * (unit * gain_row)).astype(BF)
        seed = cot[b].astype(F32) * alive
        dgain[...] += jnp.sum(seed * unit, axis=0, keepdims=True)
        seed = seed * gain_row
        grad = scale * (
            seed
            - jnp.mean(seed, axis=-1, keepdims=True)
            - unit * jnp.mean(seed * unit, axis=-1, keepdims=True)
        )
        gupd[rows_i, :] = grad.astype(BF)
        gnode[rows_i, :] = (dot_nt(gupd[rows_i, :], n2f[...]) * node_slope).astype(BF)
        back = dot_nt(gnode[rows_i, :], n1f[...])
        gxnode[rows_i, :] = back[:, :width] + cot[b].astype(F32)
        gmsg[rows_i, :] = back[:, width:].astype(BF)
        gsum[rows_i, :] = dot_nt(gmsg[rows_i, :], w2f[...]) * (0.5 * alive)

    twin_new = remote(new_mine, new_other, twin_send.at[0], twin_recv.at[0], twin)
    twin_new.start()
    ones = jnp.ones((16, own * BLOCK), BF)
    dnode = dot_tn(pair[...], gnode[...])
    dew2 = dot_tn(esum[...], gmsg[...])
    dnw2 = dot_tn(hidden[...], gupd[...])
    dnb = dot_nn(ones, gnode[...])[:1, :]
    dgain_row = dgain[...].astype(BF).astype(F32)
    for out, lo in ((reducer_n.mine, 0), (reducer_n.other, quarter)):
        hi = lo + quarter
        fill(
            out,
            columns(dnode, lo, hi) + [dew2[lo:hi, :], dnw2[lo:hi, :]],
            columns(dnb, lo, hi) + [dgain_row],
        )
    reducer_n.to_sub()

    def backward(i):
        b = core * own + i
        ids = [jnp.maximum(links[b, k], 0) for k in range(fan)]
        for k in range(fan):
            srcs[k * BLOCK : (k + 1) * BLOCK, :] = ext[ids[k]]

        @pl.loop(0, BLOCK // CHUNK)
        def _(r):
            rows = pl.ds(pl.multiple_of(i * BLOCK + r * CHUNK, CHUNK), CHUNK)
            upstream = gsum[rows, :]
            total = jnp.zeros_like(upstream)
            for k in range(fan):
                at = pl.ds(pl.multiple_of((i * fan + k) * BLOCK + r * CHUNK, CHUNK), CHUNK)
                g = upstream * slope[at, :].astype(F32)
                total = total + g
                slope[at, :] = g.astype(BF)
            tgrad[rows, :] = total.astype(BF)

        rows = pl.ds(pl.multiple_of(i * fan * BLOCK, BLOCK), fan * BLOCK)
        g = slope[rows, :]
        spread = dot_nt(g, w1f[width:, :])
        for k in range(fan):
            e = i * fan + k
            chain[e] = spread[k * BLOCK : (k + 1) * BLOCK, :] + chain[prev[e]]
        dsrc[...] += dot_tn(srcs[...], g)

    steps = [reducer_n.to_case, reducer_n.to_dom, reducer_n.to_gather, reducer_n.forward]
    for n, step in enumerate(steps):
        pl.loop(min(n, own), min(n + 1, own))(backward)
        step()
    pl.loop(min(len(steps), own), own)(backward)

    def home_copy(j, there):
        return remote(
            ghost_grad.at[j], ghost_in.at[j], home_send.at[j], home_recv.at[j], {"dom": there}
        )

    for j in (2, 3, 0, 1):
        for m in range(bound):
            ghost_grad[j, m] = chain[last[block_count + j * bound + m]].astype(BF)

        @pl.when(inside(here - DISTANCES[j], dom_count))
        def _():
            home_copy(j, here - DISTANCES[j]).start()

    dtgt = dot_tn(pair[:, :width], tgrad[...])
    deb = dot_nn(ones, tgrad[...])[:1, :]
    for out, lo in ((reducer_e.other, quarter), (reducer_e.mine, 0)):
        hi = lo + quarter
        both = zip(columns(dtgt, lo, hi), columns(dsrc[...], lo, hi))
        fill(out, [x for pieces in both for x in pieces], columns(deb, lo, hi))
        if lo > 0:
            reducer_e.to_sub()
    reducer_e.to_case()
    reducer_n.finish()

    part = psrc
    @pl.loop(0, block_count)
    def _(b):
        part[b, :, :width] = chain[last[b]]

    @pl.loop(0, own)
    def _(i):
        rows = block_rows(i)
        part[core * own + i, :, :width] += gxnode[rows, :] + dot_nt(tgrad[rows, :], w1f[:width, :])

    for j in range(4):

        @pl.when(inside(here + DISTANCES[j], dom_count))
        def _():
            home_copy(j, here + DISTANCES[j]).wait_recv()

    reducer_e.to_dom()
    hits = [
        [jnp.where(send[j, m] == b, 1.0, 0.0) for j in range(4) for m in range(bound)]
        for b in range(block_count)
    ]

    @pl.loop(0, BLOCK // CHUNK)
    def _(r):
        rows = pl.ds(pl.multiple_of(r * CHUNK, CHUNK), CHUNK)
        slots = [
            ghost_in[j, m, rows, :].astype(F32) for j in range(4) for m in range(bound)
        ]
        for b in range(block_count):
            value = part[b, rows, :width]
            for s in range(ghost_count):
                value = value + hits[b][s] * slots[s]
            node_mine[pl.ds(pl.multiple_of(b * BLOCK + r * CHUNK, CHUNK), CHUNK), :] = (
                value.astype(BF)
            )

    twin_node = remote(node_mine, node_other, twin_send.at[1], twin_recv.at[1], twin)
    twin_node.start()
    reducer_e.to_gather()
    reducer_e.forward()
    twin_new.wait()
    twin_node.wait()
    for j in range(4):

        @pl.when(inside(here - DISTANCES[j], dom_count))
        def _():
            home_copy(j, here - DISTANCES[j]).wait_send()

    reducer_e.finish()


def unpack_kernel(final_n, final_e, node_mine, node_other, new_mine, new_other, *outs):
    new_nodes, node_grads, dew1, deb, dew2, dnw1, dnb, dnw2, dgain = outs
    core = lax.axis_index("sub")
    half = new_mine.shape[0]
    new_nodes[pl.ds(pl.multiple_of(core * half, BLOCK), half), :] = new_mine[...]
    new_nodes[pl.ds(pl.multiple_of((1 - core) * half, BLOCK), half), :] = new_other[...]
    node_grads[...] = (node_mine[...].astype(F32) + node_other[...].astype(F32)).astype(BF)
    tall, quarter = dew1.shape
    ends = []
    for final, out in ((final_e, dew1), (final_n, dnw1)):
        at = 0
        for c in range(0, quarter, 128):
            out[:, c : c + 128] = final[at : at + tall, :].astype(F32)
            at += tall
        ends.append(at)
    at = ends[1]
    for out in (dew2, dnw2):
        out[...] = final_n[at : at + quarter, :].astype(F32)
        at += quarter
    tail_n = final_n[at : at + 16, :].astype(F32)
    tail_e = final_e[ends[0] : ends[0] + 16, :].astype(F32)
    n = quarter // 128
    for c in range(n):
        deb[:, c * 128 : (c + 1) * 128] = tail_e[c : c + 1, :]
        dnb[:, c * 128 : (c + 1) * 128] = tail_n[c : c + 1, :]
    dgain[...] = tail_n[n : n + 1, :]


def on_device(
    dom_count,
    case_count,
    node_feats,
    cotangent,
    block_counts,
    neighbours,
    send_sets,
    edge_w1,
    edge_b1,
    edge_w2,
    node_w1,
    node_b1,
    node_w2,
    norm_gain,
):
    _, rows, width = node_feats.shape
    block_count, fan = neighbours.shape
    bound = send_sets.shape[1]
    quarter = edge_w1.shape[1]
    wide = 2 * quarter
    ext_count = block_count + 4 * bound
    half = rows // 2
    edges = block_count // 2 * fan
    vmem = pl.BlockSpec(memory_space=pltpu.VMEM)
    smem = pl.BlockSpec(memory_space=pltpu.SMEM)
    anywhere = pl.BlockSpec(memory_space=pl.ANY)
    shape = jax.ShapeDtypeStruct
    dma = pltpu.SemaphoreType.DMA
    feats = node_feats.reshape(block_count, BLOCK, width)
    cot = cotangent.reshape(block_count, BLOCK, width)
    eb = edge_b1.reshape(1, quarter)
    nb = node_b1.reshape(1, quarter)
    gain = norm_gain.reshape(1, width)

    prev, last = pl.pallas_call(
        chain_kernel,
        out_shape=[shape((edges,), jnp.int32), shape((ext_count,), jnp.int32)],
        in_specs=[smem],
        out_specs=[smem, smem],
        name="chain",
    )(neighbours)

    def padded(count):
        unit = 16 * dom_count * case_count
        return -(-(count + 16) // unit) * unit

    def reducer_scratch(total):
        slab = total // case_count
        piece = slab // dom_count
        count = case_count + 2 * (dom_count - 1) + (case_count - 1) * dom_count
        return [
            pltpu.VMEM((total, 128), F32),
            pltpu.VMEM((total, 128), BF),
            pltpu.VMEM((total, 128), BF),
            pltpu.VMEM((case_count - 1, slab, 128), BF),
            pltpu.VMEM((case_count - 1, slab, 128), BF),
            pltpu.VMEM((slab, 128), BF),
            pltpu.VMEM((dom_count - 1, piece, 128), BF),
            dma((count,)),
            dma((count,)),
        ]

    total_n = padded(4 * quarter)
    total_e = padded(2 * quarter)
    blocks = (4, bound, BLOCK, width)
    results = pl.pallas_call(
        functools.partial(layer_kernel, dom_count, case_count, bound),
        out_shape=[
            shape((total_n, 128), BF),
            shape((total_e, 128), BF),
            shape((rows, width), BF),
            shape((rows, width), BF),
            shape((half, width), BF),
            shape((half, width), BF),
        ],
        in_specs=[smem] * 5 + [anywhere] * 9,
        out_specs=[vmem] * 6,
        scratch_shapes=reducer_scratch(total_n)
        + reducer_scratch(total_e)
        + [
            pltpu.VMEM((block_count, BLOCK, width), BF),
            pltpu.VMEM((block_count, BLOCK, width), BF),
            pltpu.VMEM((1, width), F32),
            pltpu.VMEM(blocks, BF),
            pltpu.VMEM(blocks, BF),
            pltpu.VMEM((ext_count, BLOCK, width), BF),
            pltpu.VMEM((2 * width, wide), BF),
            pltpu.VMEM((1, wide), F32),
            pltpu.VMEM((wide, width), BF),
            pltpu.VMEM((2 * width, wide), BF),
            pltpu.VMEM((1, wide), F32),
            pltpu.VMEM((wide, width), BF),
            pltpu.VMEM((2 * width, wide), BF),
            pltpu.VMEM((ext_count, BLOCK, wide), F32),
            pltpu.VMEM((BLOCK, wide), F32),
            pltpu.VMEM((edges * BLOCK, wide), BF),
            pltpu.VMEM((half, wide), F32),
            pltpu.VMEM((half, wide), BF),
            pltpu.VMEM((half, 2 * width), BF),
            pltpu.VMEM((half, wide), BF),
            pltpu.VMEM((half, width), BF),
            pltpu.VMEM((half, wide), BF),
            pltpu.VMEM((half, width), BF),
            pltpu.VMEM((half, wide), BF),
            pltpu.VMEM((half, width), F32),
            pltpu.VMEM((width, wide), F32),
            pltpu.VMEM((1, width), F32),
            pltpu.VMEM((fan * BLOCK, width), BF),
            pltpu.VMEM((edges + 1, BLOCK, width), F32),
            pltpu.VMEM(blocks, BF),
            pltpu.VMEM(blocks, BF),
            dma((9,)),
            dma((6,)),
            dma((6,)),
            dma((4,)),
            dma((4,)),
            dma((4,)),
            dma((4,)),
            dma((2,)),
            dma((2,)),
        ],
        compiler_params=pltpu.CompilerParams(
            collective_id=0, has_side_effects=True, vmem_limit_bytes=48 << 20
        ),
        name="layer",
    )(
        send_sets, block_counts, neighbours, prev, last, feats, cot, gain,
        edge_w1, eb, edge_w2, node_w1, nb, node_w2,
    )

    outs = pl.pallas_call(
        unpack_kernel,
        out_shape=[
            shape((rows, width), BF),
            shape((rows, width), BF),
            shape((2 * width, quarter), F32),
            shape((1, quarter), F32),
            shape((quarter, width), F32),
            shape((2 * width, quarter), F32),
            shape((1, quarter), F32),
            shape((quarter, width), F32),
            shape((1, width), F32),
        ],
        in_specs=[vmem] * 6,
        out_specs=[vmem] * 9,
        compiler_params=pltpu.CompilerParams(vmem_limit_bytes=16 << 20),
        name="unpack",
    )(*results)
    return (
        outs[0][None],
        outs[1][None],
        outs[2],
        outs[3].reshape(quarter),
        outs[4],
        outs[5],
        outs[6].reshape(quarter),
        outs[7],
        outs[8].reshape(width),
    )


def solution(mesh):
    placed = (
        P(("groups", "case"), "dom", None),
        P(("groups", "case"), "dom", None),
        P(("groups", "dom")),
        P(("groups", "dom"), None),
        P(("groups", "dom"), None),
        P(None, "sub"),
        P("sub"),
        P("sub", None),
        P(None, "sub"),
        P("sub"),
        P("sub", None),
        P(),
    )
    return jax.shard_map(
        functools.partial(on_device, mesh.shape["dom"], mesh.shape["case"]),
        mesh=mesh,
        in_specs=placed,
        out_specs=(
            P(("groups", "case"), "dom", None),
            P(("groups", "case"), "dom", None),
            P("groups", "sub"),
            P(("groups", "sub")),
            P(("groups", "sub"), None),
            P("groups", "sub"),
            P(("groups", "sub")),
            P(("groups", "sub"), None),
            P("groups"),
        ),
        check_vma=False,
    )
```

```python
import functools

import jax
import jax.numpy as jnp
from jax import lax
from jax.experimental import pallas as pl
from jax.experimental.pallas import tpu as pltpu
from jax.sharding import PartitionSpec as P

BLOCK = 128
CHUNK = 16
DISTANCES = (1, -1, 2, -2)
EPSILON = 1e-05
MESH = pl.DeviceIdType.MESH
BF = jnp.bfloat16
F32 = jnp.float32


def dot_nn(a, b):
    return lax.dot_general(a, b, (((1,), (0,)), ((), ())), preferred_element_type=F32)


def dot_nt(a, b):
    return lax.dot_general(a, b, (((1,), (1,)), ((), ())), preferred_element_type=F32)


def dot_tn(a, b):
    return lax.dot_general(a, b, (((0,), (0,)), ((), ())), preferred_element_type=F32)


def inside(position, count):
    return (position >= 0) & (position < count)


def remote(src, dst, send_sem, recv_sem, device):
    return pltpu.make_async_remote_copy(
        src_ref=src,
        dst_ref=dst,
        send_sem=send_sem,
        recv_sem=recv_sem,
        device_id=device,
        device_id_type=MESH,
    )


def chain_kernel(links, prev_o, last_o):
    core = lax.axis_index("sub")
    block_count, fan = links.shape
    own = block_count // 2
    none = own * fan

    for s in range(last_o.shape[0]):
        last_o[s] = none

    @pl.loop(0, own)
    def _(i):
        for k in range(fan):
            source = jnp.maximum(links[core * own + i, k], 0)
            prev_o[i * fan + k] = last_o[source]
            last_o[source] = i * fan + k


class Reducer:
    def __init__(self, dom_count, case_count, final, refs):
        (self.mine, self.other, self.twin_in, self.reduced, self.case_in, self.case_red,
         self.dom_in, self.send, self.recv) = refs
        self.final = final
        self.dom_count, self.case_count = dom_count, case_count
        self.here, self.case = lax.axis_index("dom"), lax.axis_index("case")
        self.twin = {"sub": 1 - lax.axis_index("sub")}
        self.slab = self.mine.shape[0] // case_count
        self.piece = self.slab // dom_count

    def copy(self, src, dst, n, device):
        return remote(src, dst, self.send.at[n], self.recv.at[n], device)

    def slab_rows(self, c):
        return pl.ds(pl.multiple_of(c * self.slab, 16), self.slab)

    def piece_rows(self, d):
        return pl.ds(pl.multiple_of(d * self.piece, 16), self.piece)

    def final_rows(self, c, d):
        return pl.ds(pl.multiple_of(c * self.slab + d * self.piece, 16), self.piece)

    def case_peer(self, o):
        return lax.rem(self.case + o, self.case_count)

    def dom_peer(self, o):
        return lax.rem(self.here + o, self.dom_count)

    def sub_copy(self):
        return self.copy(self.other, self.twin_in, 0, self.twin)

    def case_copy(self, o):
        return self.copy(
            self.reduced.at[o - 1], self.case_in.at[o - 1], o, {"case": self.case_peer(o)}
        )

    def dom_copy(self, o):
        peer = self.dom_peer(o)
        return self.copy(
            self.case_red.at[self.piece_rows(peer)],
            self.dom_in.at[o - 1],
            self.case_count + o - 1,
            {"dom": peer},
        )

    def dom_gather(self, o, owner, peer):
        rows = self.final_rows(self.case, owner)
        n = self.case_count + self.dom_count - 1 + o - 1
        return self.copy(self.final.at[rows], self.final.at[rows], n, {"dom": peer})

    def case_gather(self, o, oz, source):
        owner = lax.rem(self.here - oz + self.dom_count, self.dom_count)
        rows = self.final_rows(source, owner)
        n = self.case_count + 2 * (self.dom_count - 1) + (o - 1) * self.dom_count + oz
        return self.copy(
            self.final.at[rows], self.final.at[rows], n, {"case": self.case_peer(o)}
        )

    def to_sub(self):
        self.sub_copy().start()

    def to_case(self):
        self.sub_copy().wait()
        for o in range(1, self.case_count):
            rows = self.slab_rows(self.case_peer(o))
            self.reduced[o - 1] = (self.mine[rows, :] + self.twin_in[rows, :].astype(F32)).astype(BF)
            self.case_copy(o).start()

    def to_dom(self):
        for o in range(1, self.case_count):
            self.case_copy(o).wait()
        rows = self.slab_rows(self.case)
        value = self.mine[rows, :] + self.twin_in[rows, :].astype(F32)
        for o in range(1, self.case_count):
            value = value + self.case_in[o - 1].astype(F32)
        self.case_red[...] = value.astype(BF)
        for o in range(1, self.dom_count):
            self.dom_copy(o).start()

    def to_gather(self):
        for o in range(1, self.dom_count):
            self.dom_copy(o).wait()
        value = self.case_red[self.piece_rows(self.here), :].astype(F32)
        for o in range(1, self.dom_count):
            value = value + self.dom_in[o - 1].astype(F32)
        self.final[self.final_rows(self.case, self.here), :] = value.astype(BF)
        for o in range(1, self.dom_count):
            self.dom_gather(o, self.here, self.dom_peer(o)).start()
        for o in range(1, self.case_count):
            self.case_gather(o, 0, self.case).start()

    def forward(self):
        for oz in range(1, self.dom_count):
            source = lax.rem(self.here - oz + self.dom_count, self.dom_count)
            self.dom_gather(oz, source, source).wait_recv()
            for o in range(1, self.case_count):
                self.case_gather(o, oz, self.case).start()

    def finish(self):
        for o in range(1, self.dom_count):
            self.dom_gather(o, self.here, self.dom_peer(o)).wait_send()
        for oz in range(self.dom_count):
            for o in range(1, self.case_count):
                self.case_gather(o, oz, self.case).wait_send()
                source = lax.rem(self.case - o + self.case_count, self.case_count)
                self.case_gather(o, oz, source).wait_recv()


def fill(out, pieces, lines):
    at = 0
    for piece in pieces:
        out[at : at + piece.shape[0], :] = piece.astype(out.dtype)
        at += piece.shape[0]
    if lines:
        fill_lines(out, at, lines)
    elif at < out.shape[0]:
        out[at:, :] = jnp.zeros((out.shape[0] - at, 128), out.dtype)


def fill_lines(out, at, lines):
    lines = lines + [jnp.zeros((16 - len(lines), 128), F32)]
    out[at : at + 16, :] = jnp.concatenate(lines, axis=0).astype(out.dtype)
    at += 16
    if at < out.shape[0]:
        out[at:, :] = jnp.zeros((out.shape[0] - at, 128), out.dtype)


def columns(value, lo, hi):
    return [value[:, c : c + 128] for c in range(lo, hi, 128)]


def layer_kernel(dom_count, case_count, bound, *refs):
    send, counts, links, prev, last = refs[:5]
    feats_h, cot_h, gain_h = refs[5:8]
    mine = refs[8:14]
    final_n, final_e, node_mine, node_other, new_mine, new_other = refs[14:20]
    reducer_n = Reducer(dom_count, case_count, final_n, refs[20:29])
    reducer_e = Reducer(dom_count, case_count, final_e, refs[29:38])
    (
        feats, cot, gain, stage, ghosts, ext,
        w1f, ebias, w2f, n1f, nbias, n2f, w1h,
        psrc, ptgt, slope, gsum, esum, pair, hidden, gupd, gnode,
        gmsg, tgrad, gxnode, dsrc, dgain, srcs, chain, ghost_grad, ghost_in,
        local, half_send, half_recv, ghost_send, ghost_recv, home_send, home_recv,
        twin_send, twin_recv,
    ) = refs[38:]
    core = lax.axis_index("sub")
    here = lax.axis_index("dom")
    case = lax.axis_index("case")
    twin = {"sub": 1 - core}
    block_count, fan = links.shape
    width = feats.shape[2]
    quarter = mine[0].shape[1]
    wide = 2 * quarter
    own = block_count // 2
    ghost_count = 4 * bound
    none = own * fan
    left, right = pl.ds(0, quarter), pl.ds(quarter, quarter)

    def block_rows(b):
        return pl.ds(pl.multiple_of(b * BLOCK, BLOCK), BLOCK)

    def half_of(n, part):
        ref = (w1f, ebias, w2f, n1f, nbias, n2f)[n]
        return ref.at[part, :] if n in (2, 5) else ref.at[:, part]

    locals_ = [pltpu.make_async_copy(feats_h, feats, local.at[0])]
    locals_ += [pltpu.make_async_copy(mine[n], half_of(n, left), local.at[1 + n]) for n in range(6)]
    locals_ += [
        pltpu.make_async_copy(gain_h, gain, local.at[7]),
        pltpu.make_async_copy(cot_h, cot, local.at[8]),
    ]
    for copy in locals_:
        copy.start()

    barrier = pltpu.get_barrier_semaphore()
    pl.semaphore_signal(barrier, inc=1, device_id=twin, device_id_type=MESH)
    for o in range(1, dom_count):
        pl.semaphore_signal(
            barrier, inc=1, device_id={"dom": lax.rem(here + o, dom_count)}, device_id_type=MESH
        )
    for o in range(1, case_count):
        pl.semaphore_signal(
            barrier, inc=1, device_id={"case": lax.rem(case + o, case_count)}, device_id_type=MESH
        )
    locals_[0].wait()
    for j in range(4):
        for m in range(bound):
            stage[j, m] = feats[send[j, m]]
    pl.semaphore_wait(barrier, 1 + (dom_count - 1) + (case_count - 1))

    halves = [
        remote(mine[n], half_of(n, right), half_send.at[n], half_recv.at[n], twin)
        for n in range(6)
    ]
    halves[0].start()

    def ghost_copy(j, there):
        return remote(
            stage.at[j], ghosts.at[j], ghost_send.at[j], ghost_recv.at[j], {"dom": there}
        )

    for j in (2, 3, 0, 1):

        @pl.when(inside(here + DISTANCES[j], dom_count))
        def _():
            ghost_copy(j, here + DISTANCES[j]).start()

    for copy in halves[1:]:
        copy.start()
    for j in range(4):

        @pl.when(jnp.logical_not(inside(here - DISTANCES[j], dom_count)))
        def _():
            ghosts[j] = jnp.zeros(ghosts.shape[1:], BF)

        @pl.when(jnp.logical_not(inside(here + DISTANCES[j], dom_count)))
        def _():
            ghost_in[j] = jnp.zeros(ghost_in.shape[1:], BF)

    dgain[...] = jnp.zeros_like(dgain)
    dsrc[...] = jnp.zeros_like(dsrc)
    chain[none] = jnp.zeros(chain.shape[1:], F32)
    for copy in locals_[1:]:
        copy.wait()
    halves[0].wait()
    w1h[...] = w1f[...] * jnp.asarray(0.5, BF)

    @pl.loop(0, block_count)
    def _(b):
        ext[b] = feats[b]
        psrc[b] = dot_nn(feats[b], w1h[width:, :])

    for copy in halves[1:]:
        copy.wait()
    edge_bias = ebias[...] * 0.5
    node_bias = nbias[...]
    gain_row = gain[...]
    for j in range(4):

        @pl.when(inside(here - DISTANCES[j], dom_count))
        def _():
            ghost_copy(j, here - DISTANCES[j]).wait_recv()

        @pl.when(inside(here + DISTANCES[j], dom_count))
        def _():
            ghost_copy(j, here + DISTANCES[j]).wait_send()

        for m in range(bound):
            s = block_count + j * bound + m
            ext[s] = ghosts[j, m]
            psrc[s] = dot_nn(ghosts[j, m], w1h[width:, :])

    @pl.loop(0, own)
    def _(i):
        b = core * own + i
        alive = jnp.where(b < counts[0], 1.0, 0.0)
        ids = [jnp.maximum(links[b, k], 0) for k in range(fan)]
        rows_i = block_rows(i)
        targets = feats[b]
        ptgt[...] = dot_nn(targets, w1h[:width, :]) + edge_bias

        @pl.loop(0, BLOCK // CHUNK)
        def _(r):
            rows = pl.ds(pl.multiple_of(r * CHUNK, CHUNK), CHUNK)
            base = ptgt[rows, :]
            total = jnp.zeros_like(base)
            for k in range(fan):
                h = psrc[ids[k], rows, :] + base
                t = jnp.tanh(h)
                a = 1.0 + t
                q = h * a
                total = total + q
                at = pl.multiple_of((i * fan + k) * BLOCK + r * CHUNK, CHUNK)
                slope[pl.ds(at, CHUNK), :] = (a + q * (1.0 - t)).astype(BF)
            esum[pl.ds(pl.multiple_of(i * BLOCK + r * CHUNK, CHUNK), CHUNK), :] = (
                total * alive
            ).astype(BF)

        message = dot_nn(esum[rows_i, :], w2f[...]).astype(BF)
        pair[rows_i, :width] = targets
        pair[rows_i, width:] = message
        h = (dot_nn(pair[rows_i, :], n1f[...]) + node_bias) * 0.5
        t = jnp.tanh(h)
        a = 1.0 + t
        q = h * a
        node_slope = 0.5 * (a + q * (1.0 - t))
        hidden[rows_i, :] = q.astype(BF)
        update = dot_nn(hidden[rows_i, :], n2f[...])
        shifted = update - jnp.mean(update, axis=-1, keepdims=True)
        spread = jnp.mean(shifted * shifted, axis=-1, keepdims=True)
        scale = lax.rsqrt(spread + EPSILON)
        unit = shifted * scale
        new_mine[rows_i, :] = (targets.astype(F32) + alive * (unit * gain_row)).astype(BF)
        seed = cot[b].astype(F32) * alive
        dgain[...] += jnp.sum(seed * unit, axis=0, keepdims=True)
        seed = seed * gain_row
        grad = scale * (
            seed
            - jnp.mean(seed, axis=-1, keepdims=True)
            - unit * jnp.mean(seed * unit, axis=-1, keepdims=True)
        )
        gupd[rows_i, :] = grad.astype(BF)
        gnode[rows_i, :] = (dot_nt(gupd[rows_i, :], n2f[...]) * node_slope).astype(BF)
        back = dot_nt(gnode[rows_i, :], n1f[...])
        gxnode[rows_i, :] = back[:, :width] + cot[b].astype(F32)
        gmsg[rows_i, :] = back[:, width:].astype(BF)
        gsum[rows_i, :] = dot_nt(gmsg[rows_i, :], w2f[...]) * (0.5 * alive)

    twin_new = remote(new_mine, new_other, twin_send.at[0], twin_recv.at[0], twin)
    twin_new.start()
    ones = jnp.ones((16, own * BLOCK), BF)
    dnode = dot_tn(pair[...], gnode[...])
    dew2 = dot_tn(esum[...], gmsg[...])
    dnw2 = dot_tn(hidden[...], gupd[...])
    dnb = dot_nn(ones, gnode[...])[:1, :]
    dgain_row = dgain[...].astype(BF).astype(F32)
    for out, lo in ((reducer_n.mine, 0), (reducer_n.other, quarter)):
        hi = lo + quarter
        fill(
            out,
            columns(dnode, lo, hi) + [dew2[lo:hi, :], dnw2[lo:hi, :]],
            [],
        )
    reducer_n.to_sub()

    def backward(i):
        b = core * own + i
        ids = [jnp.maximum(links[b, k], 0) for k in range(fan)]
        for k in range(fan):
            srcs[k * BLOCK : (k + 1) * BLOCK, :] = ext[ids[k]]

        @pl.loop(0, BLOCK // CHUNK)
        def _(r):
            rows = pl.ds(pl.multiple_of(i * BLOCK + r * CHUNK, CHUNK), CHUNK)
            upstream = gsum[rows, :]
            total = jnp.zeros_like(upstream)
            for k in range(fan):
                at = pl.ds(pl.multiple_of((i * fan + k) * BLOCK + r * CHUNK, CHUNK), CHUNK)
                g = upstream * slope[at, :].astype(F32)
                total = total + g
                slope[at, :] = g.astype(BF)
            tgrad[rows, :] = total.astype(BF)

        rows = pl.ds(pl.multiple_of(i * fan * BLOCK, BLOCK), fan * BLOCK)
        g = slope[rows, :]
        spread = dot_nt(g, w1f[width:, :])
        for k in range(fan):
            e = i * fan + k
            chain[e] = spread[k * BLOCK : (k + 1) * BLOCK, :] + chain[prev[e]]
        dsrc[...] += dot_tn(srcs[...], g)

    first = min(2, own)
    pl.loop(0, first)(backward)
    reducer_n.to_case()
    pl.loop(first, own)(backward)

    def home_copy(j, there):
        return remote(
            ghost_grad.at[j], ghost_in.at[j], home_send.at[j], home_recv.at[j], {"dom": there}
        )

    for j in (2, 3, 0, 1):
        for m in range(bound):
            ghost_grad[j, m] = chain[last[block_count + j * bound + m]].astype(BF)

        @pl.when(inside(here - DISTANCES[j], dom_count))
        def _():
            home_copy(j, here - DISTANCES[j]).start()

    dtgt = dot_tn(pair[:, :width], tgrad[...])
    deb = dot_nn(ones, tgrad[...])[:1, :]
    for out, lo in ((reducer_e.other, quarter), (reducer_e.mine, 0)):
        hi = lo + quarter
        both = zip(columns(dtgt, lo, hi), columns(dsrc[...], lo, hi))
        lines = columns(deb, lo, hi) + columns(dnb, lo, hi) + [dgain_row]
        fill(out, [x for pieces in both for x in pieces], lines)
        if lo > 0:
            reducer_e.to_sub()
    reducer_n.to_dom()
    part = psrc

    @pl.loop(0, block_count)
    def _(b):
        part[b, :, :width] = chain[last[b]]

    @pl.loop(0, own)
    def _(i):
        rows = block_rows(i)
        part[core * own + i, :, :width] += gxnode[rows, :] + dot_nt(tgrad[rows, :], w1f[:width, :])

    reducer_e.to_case()
    reducer_n.to_gather()
    for j in range(4):

        @pl.when(inside(here + DISTANCES[j], dom_count))
        def _():
            home_copy(j, here + DISTANCES[j]).wait_recv()

    hits = [
        [jnp.where(send[j, m] == b, 1.0, 0.0) for j in range(4) for m in range(bound)]
        for b in range(block_count)
    ]

    @pl.loop(0, BLOCK // CHUNK)
    def _(r):
        rows = pl.ds(pl.multiple_of(r * CHUNK, CHUNK), CHUNK)
        slots = [
            ghost_in[j, m, rows, :].astype(F32) for j in range(4) for m in range(bound)
        ]
        for b in range(block_count):
            value = part[b, rows, :width]
            for s in range(ghost_count):
                value = value + hits[b][s] * slots[s]
            node_mine[pl.ds(pl.multiple_of(b * BLOCK + r * CHUNK, CHUNK), CHUNK), :] = (
                value.astype(BF)
            )

    twin_node = remote(node_mine, node_other, twin_send.at[1], twin_recv.at[1], twin)
    twin_node.start()
    reducer_e.to_dom()
    reducer_n.forward()
    reducer_e.to_gather()
    reducer_e.forward()
    reducer_n.finish()
    twin_new.wait()
    twin_node.wait()
    for j in range(4):

        @pl.when(inside(here - DISTANCES[j], dom_count))
        def _():
            home_copy(j, here - DISTANCES[j]).wait_send()

    reducer_e.finish()


def unpack_kernel(final_n, final_e, node_mine, node_other, new_mine, new_other, *outs):
    new_nodes, node_grads, dew1, deb, dew2, dnw1, dnb, dnw2, dgain = outs
    core = lax.axis_index("sub")
    half = new_mine.shape[0]
    new_nodes[pl.ds(pl.multiple_of(core * half, BLOCK), half), :] = new_mine[...]
    new_nodes[pl.ds(pl.multiple_of((1 - core) * half, BLOCK), half), :] = new_other[...]
    node_grads[...] = (node_mine[...].astype(F32) + node_other[...].astype(F32)).astype(BF)
    tall, quarter = dew1.shape
    ends = []
    for final, out in ((final_e, dew1), (final_n, dnw1)):
        at = 0
        for c in range(0, quarter, 128):
            out[:, c : c + 128] = final[at : at + tall, :].astype(F32)
            at += tall
        ends.append(at)
    at = ends[1]
    tail = final_e[ends[0] : ends[0] + 16, :].astype(F32)
    for out in (dew2, dnw2):
        out[...] = final_n[at : at + quarter, :].astype(F32)
        at += quarter
    n = quarter // 128
    for c in range(n):
        deb[:, c * 128 : (c + 1) * 128] = tail[c : c + 1, :]
        dnb[:, c * 128 : (c + 1) * 128] = tail[n + c : n + c + 1, :]
    dgain[...] = tail[2 * n : 2 * n + 1, :]


def on_device(
    dom_count,
    case_count,
    node_feats,
    cotangent,
    block_counts,
    neighbours,
    send_sets,
    edge_w1,
    edge_b1,
    edge_w2,
    node_w1,
    node_b1,
    node_w2,
    norm_gain,
):
    _, rows, width = node_feats.shape
    block_count, fan = neighbours.shape
    bound = send_sets.shape[1]
    quarter = edge_w1.shape[1]
    wide = 2 * quarter
    ext_count = block_count + 4 * bound
    half = rows // 2
    edges = block_count // 2 * fan
    vmem = pl.BlockSpec(memory_space=pltpu.VMEM)
    smem = pl.BlockSpec(memory_space=pltpu.SMEM)
    anywhere = pl.BlockSpec(memory_space=pl.ANY)
    shape = jax.ShapeDtypeStruct
    dma = pltpu.SemaphoreType.DMA
    feats = node_feats.reshape(block_count, BLOCK, width)
    cot = cotangent.reshape(block_count, BLOCK, width)
    eb = edge_b1.reshape(1, quarter)
    nb = node_b1.reshape(1, quarter)
    gain = norm_gain.reshape(1, width)

    prev, last = pl.pallas_call(
        chain_kernel,
        out_shape=[shape((edges,), jnp.int32), shape((ext_count,), jnp.int32)],
        in_specs=[smem],
        out_specs=[smem, smem],
        name="chain",
    )(neighbours)

    def padded(count):
        unit = 16 * dom_count * case_count
        return -(-count // unit) * unit

    def reducer_scratch(total):
        slab = total // case_count
        piece = slab // dom_count
        count = case_count + 2 * (dom_count - 1) + (case_count - 1) * dom_count
        return [
            pltpu.VMEM((total, 128), F32),
            pltpu.VMEM((total, 128), BF),
            pltpu.VMEM((total, 128), BF),
            pltpu.VMEM((case_count - 1, slab, 128), BF),
            pltpu.VMEM((case_count - 1, slab, 128), BF),
            pltpu.VMEM((slab, 128), BF),
            pltpu.VMEM((dom_count - 1, piece, 128), BF),
            dma((count,)),
            dma((count,)),
        ]

    total_n = padded(2 * width * quarter // 128 + 2 * quarter)
    total_e = padded(2 * width * quarter // 128 + 16)
    blocks = (4, bound, BLOCK, width)
    results = pl.pallas_call(
        functools.partial(layer_kernel, dom_count, case_count, bound),
        out_shape=[
            shape((total_n, 128), BF),
            shape((total_e, 128), BF),
            shape((rows, width), BF),
            shape((rows, width), BF),
            shape((half, width), BF),
            shape((half, width), BF),
        ],
        in_specs=[smem] * 5 + [anywhere] * 9,
        out_specs=[vmem] * 6,
        scratch_shapes=reducer_scratch(total_n)
        + reducer_scratch(total_e)
        + [
            pltpu.VMEM((block_count, BLOCK, width), BF),
            pltpu.VMEM((block_count, BLOCK, width), BF),
            pltpu.VMEM((1, width), F32),
            pltpu.VMEM(blocks, BF),
            pltpu.VMEM(blocks, BF),
            pltpu.VMEM((ext_count, BLOCK, width), BF),
            pltpu.VMEM((2 * width, wide), BF),
            pltpu.VMEM((1, wide), F32),
            pltpu.VMEM((wide, width), BF),
            pltpu.VMEM((2 * width, wide), BF),
            pltpu.VMEM((1, wide), F32),
            pltpu.VMEM((wide, width), BF),
            pltpu.VMEM((2 * width, wide), BF),
            pltpu.VMEM((ext_count, BLOCK, wide), F32),
            pltpu.VMEM((BLOCK, wide), F32),
            pltpu.VMEM((edges * BLOCK, wide), BF),
            pltpu.VMEM((half, wide), F32),
            pltpu.VMEM((half, wide), BF),
            pltpu.VMEM((half, 2 * width), BF),
            pltpu.VMEM((half, wide), BF),
            pltpu.VMEM((half, width), BF),
            pltpu.VMEM((half, wide), BF),
            pltpu.VMEM((half, width), BF),
            pltpu.VMEM((half, wide), BF),
            pltpu.VMEM((half, width), F32),
            pltpu.VMEM((width, wide), F32),
            pltpu.VMEM((1, width), F32),
            pltpu.VMEM((fan * BLOCK, width), BF),
            pltpu.VMEM((edges + 1, BLOCK, width), F32),
            pltpu.VMEM(blocks, BF),
            pltpu.VMEM(blocks, BF),
            dma((9,)),
            dma((6,)),
            dma((6,)),
            dma((4,)),
            dma((4,)),
            dma((4,)),
            dma((4,)),
            dma((2,)),
            dma((2,)),
        ],
        compiler_params=pltpu.CompilerParams(
            collective_id=0, has_side_effects=True, vmem_limit_bytes=48 << 20
        ),
        name="layer",
    )(
        send_sets, block_counts, neighbours, prev, last, feats, cot, gain,
        edge_w1, eb, edge_w2, node_w1, nb, node_w2,
    )

    outs = pl.pallas_call(
        unpack_kernel,
        out_shape=[
            shape((rows, width), BF),
            shape((rows, width), BF),
            shape((2 * width, quarter), F32),
            shape((1, quarter), F32),
            shape((quarter, width), F32),
            shape((2 * width, quarter), F32),
            shape((1, quarter), F32),
            shape((quarter, width), F32),
            shape((1, width), F32),
        ],
        in_specs=[vmem] * 6,
        out_specs=[vmem] * 9,
        compiler_params=pltpu.CompilerParams(vmem_limit_bytes=16 << 20),
        name="unpack",
    )(*results)
    return (
        outs[0][None],
        outs[1][None],
        outs[2],
        outs[3].reshape(quarter),
        outs[4],
        outs[5],
        outs[6].reshape(quarter),
        outs[7],
        outs[8].reshape(width),
    )


def solution(mesh):
    placed = (
        P(("groups", "case"), "dom", None),
        P(("groups", "case"), "dom", None),
        P(("groups", "dom")),
        P(("groups", "dom"), None),
        P(("groups", "dom"), None),
        P(None, "sub"),
        P("sub"),
        P("sub", None),
        P(None, "sub"),
        P("sub"),
        P("sub", None),
        P(),
    )
    return jax.shard_map(
        functools.partial(on_device, mesh.shape["dom"], mesh.shape["case"]),
        mesh=mesh,
        in_specs=placed,
        out_specs=(
            P(("groups", "case"), "dom", None),
            P(("groups", "case"), "dom", None),
            P("groups", "sub"),
            P(("groups", "sub")),
            P(("groups", "sub"), None),
            P("groups", "sub"),
            P(("groups", "sub")),
            P(("groups", "sub"), None),
            P("groups"),
        ),
        check_vma=False,
    )
```
